128 devices in a mesh: peer: 2 (over core), row: 16 (over y, x), col: 4 (over z).
Axes of the slice: x: 4, y: 4, z: 4, core: 2. Of those that a mesh axis runs over, the one named last changes fastest.
Arguments:
- block_in: bfloat16 [2, 768, 7168], P('peer', 'row', 'col'), may hold values from -6 to 6
- weight_in: bfloat16 [2, 7168, 14336], P('peer', 'col', 'row'), may hold values from -0.0625 to 0.0625
- weight_out: bfloat16 [2, 14336, 7168], P('peer', 'row', 'col'), may hold values from -0.046875 to 0.046875
- upstream: bfloat16 [2, 768, 7168], P('peer', 'row', 'col'), may hold values from -6 to 6
- stale_out: bfloat16 [2, 768, 7168], P('peer', 'row', 'col'), may hold values from -6 to 6
Outputs:
- block_out: bfloat16 [2, 768, 7168], P('peer', 'row', 'col')
- grad_block_in: bfloat16 [2, 768, 7168], P('peer', 'row', 'col')
- grad_weight_in: bfloat16 [2, 7168, 14336], P('peer', 'col', 'row')
- grad_weight_out: bfloat16 [2, 14336, 7168], P('peer', 'row', 'col')
The draws below stay inside these ranges and needn't reach their ends.
All inputs are finite; a program needn't handle non-finite values.
Results may differ from the reference program's by a relative error of at most 0.024.
Values may be sent and summed in bfloat16 or wider, within the bound.
A program may use at most 128 MiB of HBM per device.

```python
import jax
import jax.numpy as jnp
from jax import lax

D = 7168
FF = 14336
TOKENS = 768
N_ROW = 16
N_COL = 4


def levels(key, extent, pieces, least, largest):
    factor_of = 1.0
    for dim, parts in pieces:
        draws = jax.random.uniform(jax.random.fold_in(jax.random.fold_in(key, 6), dim), (parts,), jnp.float32, least / len(pieces), largest / len(pieces))
        factor_of = factor_of * jnp.repeat(jnp.exp(draws), extent[dim] // parts).reshape((-1,) + (1,) * (len(extent) - 1 - dim))
    return factor_of


def gaussian(own_key, dims, scale, most, split=(), held_as=jnp.bfloat16):
    values = scale * jax.random.normal(own_key, dims, jnp.float32)
    if split:
        values = values * levels(own_key, dims, split, -0.22, 0.18)
    return jnp.clip(values, -most, most).astype(held_as)


def setup_inputs(seed: int = 0) -> dict:
    streams_of = jax.random.split(jax.random.key(seed), 6)
    return {
        "block_in": gaussian(streams_of[0], (2, TOKENS, D), 1.0, 6.0, ((0, 2), (1, 16), (2, 4))),
        "weight_in": gaussian(streams_of[1], (2, D, FF), D ** -0.5, 0.0625, ((0, 2), (1, 4), (2, 16))),
        "weight_out": gaussian(streams_of[2], (2, FF, D), FF ** -0.5, 0.046875, ((0, 2), (1, 16), (2, 4))),
        "upstream": gaussian(streams_of[3], (2, TOKENS, D), 1.0, 6.0, ((0, 2), (1, 16), (2, 4))),
        "stale_out": gaussian(streams_of[4], (2, TOKENS, D), 1.0, 6.0, ((0, 2), (1, 16), (2, 4))),
    }


feature_weight = 1.0

def gelu_value(values):
    return jax.nn.gelu(values, approximate=True)

def gelu_slope(values, cotangent):
    _, pull = jax.vjp(gelu_value, values)
    return pull(cotangent)[0]

def block_sum(left, right, count, flipped):
    width = left.shape[1] // count
    total = None
    for index in range(count):
        piece = left[:, index * width:(index + 1) * width]
        if flipped:
            weight = right[:, index * width:(index + 1) * width]
            term = jnp.dot(piece, weight.T, preferred_element_type=jnp.float32)
        else:
            weight = right[index * width:(index + 1) * width, :]
            term = jnp.dot(piece, weight, preferred_element_type=jnp.float32)
        rounded = lax.optimization_barrier(term.astype(jnp.bfloat16)).astype(jnp.float32)
        total = rounded if total is None else total + rounded
    return total

def reference(block_in, weight_in, weight_out, upstream, stale_out):
    outputs = []
    grads_in = []
    grads_first = []
    grads_second = []
    for peer_index in range(2):
        inputs = block_in[peer_index]
        w_first = weight_in[peer_index]
        w_second = weight_out[peer_index]
        cotan = upstream[peer_index]
        stale_other = stale_out[1 - peer_index]
        pre = block_sum(inputs, w_first, N_COL, False)
        hidden = gelu_value(pre).astype(jnp.bfloat16)
        output = (inputs.astype(jnp.float32) + block_sum(hidden, w_second, N_ROW, False)).astype(jnp.bfloat16)
        slope = (cotan.astype(jnp.float32) + feature_weight * (output.astype(jnp.float32) - stale_other.astype(jnp.float32))).astype(jnp.bfloat16)
        back = block_sum(slope, w_second, N_COL, True)
        inner = gelu_slope(pre, back).astype(jnp.bfloat16)
        grad_in = (slope.astype(jnp.float32) + block_sum(inner, w_first, N_ROW, True)).astype(jnp.bfloat16)
        grad_first = jnp.dot(inputs.T, inner, preferred_element_type=jnp.float32).astype(jnp.bfloat16)
        grad_second = jnp.dot(hidden.T, slope, preferred_element_type=jnp.float32).astype(jnp.bfloat16)
        outputs.append(output)
        grads_in.append(grad_in)
        grads_first.append(grad_first)
        grads_second.append(grad_second)
    return (jnp.stack(outputs), jnp.stack(grads_in), jnp.stack(grads_first), jnp.stack(grads_second))
```

```python
import functools

import jax
import jax.numpy as jnp
from jax import lax
from jax.experimental import pallas as pl
from jax.experimental.pallas import tpu as pltpu
from jax.sharding import PartitionSpec as P

feature_weight = 1.0
SIDE = 4
CHUNKS = 3
LAG = 1
STEPS = 12
MESH = pl.DeviceIdType.MESH
F32 = jnp.float32
BF16 = jnp.bfloat16


def gelu_both(v):
    inner = 0.7978845608 * (v + 0.044715 * v * v * v)
    t = jnp.tanh(inner)
    half = 0.5 * (1.0 + t)
    value = v * half
    slope = half + 0.5 * v * (1.0 - t * t) * (0.7978845608 * (1.0 + 3.0 * 0.044715 * v * v))
    return value, slope


def column_tiles(width, run):
    full = width // 256

    def step(n, carry):
        run(pl.multiple_of(n * 256, 256), 256)
        return carry

    lax.fori_loop(0, full, step, 0)
    if width % 256:
        run(full * 256, width % 256)


def kernel(
    x_ref, g_ref, s_ref, w1_ref, w2_ref,
    out_ref, gin_ref, gw1_ref, gw2_ref,
    w1, w2, stale, x_all, slope_all, hidden_all, inner_all, dgelu,
    part1, part2, got_z1, got_z2, outp, ginp,
    big_a, big_b, sum_a, sum_b, small_a, small_b, gw1, gw2,
    send_sem, recv_sem, stale_sem, local_sem, out_sem,
):
    tokens = x_ref.shape[0] // CHUNKS
    wide, units = w1.shape
    half = wide // 2
    rows = tokens * SIDE * SIDE
    left, right = pl.ds(0, half), pl.ds(half, half)
    peer, row, z = lax.axis_index("peer"), lax.axis_index("row"), lax.axis_index("col")
    y, x = lax.div(row, SIDE), lax.rem(row, SIDE)

    def at(axis, d):
        if axis == "x":
            return lax.rem(x + d, SIDE)
        if axis == "y":
            return lax.rem(y + d, SIDE)
        return lax.rem(z + d, SIDE)

    def device(axis, d):
        if axis == "x":
            return (peer, y * SIDE + at("x", d), z)
        if axis == "y":
            return (peer, at("y", d) * SIDE + x, z)
        return (peer, row, at("z", d))

    other = (1 - peer, row, z)

    load1 = pltpu.make_async_copy(w1_ref, w1, local_sem.at[0])
    load2 = pltpu.make_async_copy(w2_ref, w2, local_sem.at[1])
    load1.start()
    load2.start()

    barrier = pltpu.get_barrier_semaphore()
    for axis in "xyz":
        for d in range(1, SIDE):
            pl.semaphore_signal(barrier, inc=1, device_id=device(axis, d), device_id_type=MESH)
    pl.semaphore_signal(barrier, inc=1, device_id=other, device_id_type=MESH)
    for k in range(CHUNKS):
        x_all[k, y, x] = x_ref[pl.ds(k * tokens, tokens), :]
    pl.semaphore_wait(barrier, 3 * (SIDE - 1) + 1)

    flights = {}

    def send(k, e, src, dst, target):
        held = flights.setdefault((k, e), [])
        copy = pltpu.make_async_remote_copy(
            src_ref=src,
            dst_ref=dst,
            send_sem=send_sem.at[k, e, len(held)],
            recv_sem=recv_sem.at[k, e, len(held)],
            device_id=target,
            device_id_type=MESH,
        )
        copy.start()
        held.append(copy)

    def arrive(k, e):
        for copy in flights[k, e]:
            copy.wait_recv()

    ring = range(1, SIDE)

    def gather_first(k, e, buf):
        for d in ring:
            send(k, e, buf.at[k, y, x, :, left], buf.at[k, y, x, :, left], device("x", d))
            send(k, e, buf.at[k, y, x, :, right], buf.at[k, y, x, :, right], device("y", d))

    def gather_second(k, e, buf):
        arrive(k, e - 1)
        for d in ring:
            send(k, e, buf.at[k, y, :, :, left], buf.at[k, y, :, :, left], device("y", d))
            send(k, e, buf.at[k, :, x, :, right], buf.at[k, :, x, :, right], device("x", d))

    def scatter_left(k, e, i, buf):
        for d in ring:
            send(k, e, buf.at[k, at("y", d), :, :, left], big_a.at[i, k, d - 1], device("y", d))

    def scatter_right(k, e, i, buf):
        for d in ring:
            send(k, e, buf.at[k, :, at("x", d), :, right], big_b.at[i, k, d - 1], device("x", d))

    def scatter_second(k, e, i, buf):
        arrive(k, e - 1)
        for n in range(SIDE):
            total = buf[k, y, n, :, left].astype(F32)
            for d in ring:
                total = total + big_a[i, k, d - 1, n].astype(F32)
            sum_a[i, k, n] = total.astype(BF16)
        for d in ring:
            send(k, e, sum_a.at[i, k, at("x", d)], small_a.at[i, k, d - 1], device("x", d))
        for n in range(SIDE):
            total = buf[k, n, x, :, right].astype(F32)
            for d in ring:
                total = total + big_b[i, k, d - 1, n].astype(F32)
            sum_b[i, k, n] = total.astype(BF16)
        for d in ring:
            send(k, e, sum_b.at[i, k, at("y", d)], small_b.at[i, k, d - 1], device("y", d))

    def scatter_total(k, e, i):
        arrive(k, e - 1)
        a = sum_a[i, k, x].astype(F32)
        b = sum_b[i, k, y].astype(F32)
        for d in ring:
            a = a + small_a[i, k, d - 1].astype(F32)
            b = b + small_b[i, k, d - 1].astype(F32)
        return (left, a), (right, b)

    def col_scatter(k, e, buf, got):
        for d in ring:
            send(k, e, buf.at[k, at("z", d)], got.at[k, d - 1], device("z", d))

    def col_total(k, e, buf, got):
        arrive(k, e - 1)
        total = buf[k, z].astype(F32)
        for d in ring:
            total = total + got[k, d - 1].astype(F32)
        return total

    def col_gather(k, e, buf):
        for d in ring:
            send(k, e, buf.at[k, z], buf.at[k, z], device("z", d))

    def to_units(k, src, weight, flipped, dst):
        def tile(start, size):
            block = src[k].reshape(rows, wide)
            if flipped:
                value = lax.dot_general(
                    block, weight[pl.ds(start, size), :], (((1,), (1,)), ((), ())),
                    preferred_element_type=F32,
                )
            else:
                value = jnp.dot(block, weight[:, pl.ds(start, size)], preferred_element_type=F32)
            dst[k, :, :, pl.ds(start, size)] = value.astype(BF16).reshape(SIDE, rows // SIDE, size)

        column_tiles(units, tile)

    def to_features(k, src, weight, flipped, dst, base):
        def tile(offset, size):
            start = base + offset
            if not isinstance(start, int):
                start = pl.multiple_of(start, 128)
            block = src[k].reshape(rows, units)
            if flipped:
                value = lax.dot_general(
                    block, weight[pl.ds(start, size), :], (((1,), (1,)), ((), ())),
                    preferred_element_type=F32,
                )
            else:
                value = jnp.dot(block, weight[:, pl.ds(start, size)], preferred_element_type=F32)
            dst[k, :, :, :, pl.ds(start, size)] = value.astype(BF16).reshape(
                SIDE, SIDE, tokens, size
            )

        column_tiles(half, tile)

    def local(k):
        return pl.ds(k * tokens, tokens)

    everyone = CHUNKS * rows

    def weight_gradient(narrow, other_all, result, width):
        def tile(start, size):
            a = narrow[..., pl.ds(start, size)].reshape(everyone, size)
            b = other_all[...].reshape(everyone, width)
            result[pl.ds(start, size), :] = lax.dot_general(
                a, b, (((0,), (0,)), ((), ())), preferred_element_type=F32
            ).astype(BF16)

        return tile

    def event(k, e):
        if e == 0:
            gather_first(k, e, x_all)
        elif e == 1:
            gather_second(k, e, x_all)
        elif e == 2:
            arrive(k, e - 1)
            if k == 0:
                load1.wait()
            to_units(k, x_all, w1, False, part1)
            col_scatter(k, e, part1, got_z1)
        elif e == 3:
            value, slope = gelu_both(col_total(k, e, part1, got_z1))
            hidden_all[k, z] = value.astype(BF16)
            col_gather(k, e, hidden_all)
            dgelu[k] = slope
        elif e == 4:
            arrive(k, e - 1)
            if k == 0:
                load2.wait()
            to_features(k, hidden_all, w2, False, outp, 0)
            scatter_left(k, e, 0, outp)
            to_features(k, hidden_all, w2, False, outp, half)
            scatter_right(k, e, 0, outp)
        elif e == 5:
            scatter_second(k, e, 0, outp)
        elif e == 6:
            if k == 0:
                swap.wait_recv()
            for cols, total in scatter_total(k, e, 0):
                output = (x_ref[local(k), cols].astype(F32) + total).astype(BF16)
                out_ref[local(k), cols] = output
                slope = g_ref[local(k), cols].astype(F32) + feature_weight * (
                    output.astype(F32) - stale[local(k), cols].astype(F32)
                )
                slope_all[k, y, x, :, cols] = slope.astype(BF16)
            gather_first(k, e, slope_all)
        elif e == 7:
            gather_second(k, e, slope_all)
        elif e == 8:
            arrive(k, e - 1)
            to_units(k, slope_all, w2, True, part2)
            col_scatter(k, e, part2, got_z2)
            if k == CHUNKS - 1:
                column_tiles(units, weight_gradient(hidden_all, slope_all, gw2, wide))
                save2.start()
        elif e == 9:
            inner = col_total(k, e, part2, got_z2) * dgelu[k]
            inner_all[k, z] = inner.astype(BF16)
            col_gather(k, e, inner_all)
        elif e == 10:
            arrive(k, e - 1)
            to_features(k, inner_all, w1, True, ginp, 0)
            scatter_left(k, e, 1, ginp)
            to_features(k, inner_all, w1, True, ginp, half)
            scatter_right(k, e, 1, ginp)
            if k == CHUNKS - 1:
                column_tiles(wide, weight_gradient(x_all, inner_all, gw1, units))
                save1.start()
        elif e == 11:
            scatter_second(k, e, 1, ginp)
        elif e == 12:
            for cols, total in scatter_total(k, e, 1):
                mine = slope_all[k, y, x, :, cols].astype(F32)
                gin_ref[local(k), cols] = (mine + total).astype(BF16)

    swap = pltpu.make_async_remote_copy(
        src_ref=s_ref, dst_ref=stale, send_sem=stale_sem.at[0], recv_sem=stale_sem.at[1],
        device_id=other, device_id_type=MESH,
    )
    save1 = pltpu.make_async_copy(gw1, gw1_ref, out_sem.at[0])
    save2 = pltpu.make_async_copy(gw2, gw2_ref, out_sem.at[1])

    for tick in range(STEPS + 1 + LAG * (CHUNKS - 1)):
        for k in range(CHUNKS):
            e = tick - LAG * k
            if 0 <= e <= STEPS:
                event(k, e)
        if tick == 0:
            swap.start()
    swap.wait_send()
    for held in flights.values():
        for copy in held:
            copy.wait_send()
    save2.wait()
    save1.wait()


def body(block_in, weight_in, weight_out, upstream, stale_out):
    x, w1, w2, g, s = block_in[0], weight_in[0], weight_out[0], upstream[0], stale_out[0]
    wide, units = w1.shape
    own = x.shape[0]
    tokens = own // CHUNKS
    rows = tokens * SIDE * SIDE
    half = wide // 2
    share = rows // SIDE
    ring = SIDE - 1
    inside = pl.BlockSpec(memory_space=pltpu.VMEM)
    anywhere = pl.BlockSpec(memory_space=pl.ANY)
    row_all = pltpu.VMEM((CHUNKS, SIDE, SIDE, tokens, wide), BF16)
    col_all = pltpu.VMEM((CHUNKS, SIDE, share, units), BF16)
    col_got = pltpu.VMEM((CHUNKS, ring, share, units), BF16)
    flops = 12 * own * 16 * wide * units
    out, gin, gw1, gw2 = pl.pallas_call(
        kernel,
        out_shape=(
            jax.ShapeDtypeStruct(x.shape, BF16),
            jax.ShapeDtypeStruct(x.shape, BF16),
            jax.ShapeDtypeStruct(w1.shape, BF16),
            jax.ShapeDtypeStruct(w2.shape, BF16),
        ),
        in_specs=[inside, inside, inside, anywhere, anywhere],
        out_specs=(inside, inside, anywhere, anywhere),
        scratch_shapes=[
            pltpu.VMEM((wide, units), BF16),
            pltpu.VMEM((units, wide), BF16),
            pltpu.VMEM(x.shape, BF16),
            row_all,
            row_all,
            col_all,
            col_all,
            pltpu.VMEM((CHUNKS, share, units), F32),
            col_all,
            col_all,
            col_got,
            col_got,
            row_all,
            row_all,
            pltpu.VMEM((2, CHUNKS, ring, SIDE, tokens, half), BF16),
            pltpu.VMEM((2, CHUNKS, ring, SIDE, tokens, half), BF16),
            pltpu.VMEM((2, CHUNKS, SIDE, tokens, half), BF16),
            pltpu.VMEM((2, CHUNKS, SIDE, tokens, half), BF16),
            pltpu.VMEM((2, CHUNKS, ring, tokens, half), BF16),
            pltpu.VMEM((2, CHUNKS, ring, tokens, half), BF16),
            pltpu.VMEM((wide, units), BF16),
            pltpu.VMEM((units, wide), BF16),
            pltpu.SemaphoreType.DMA((CHUNKS, STEPS, 2 * ring)),
            pltpu.SemaphoreType.DMA((CHUNKS, STEPS, 2 * ring)),
            pltpu.SemaphoreType.DMA((2,)),
            pltpu.SemaphoreType.DMA((2,)),
            pltpu.SemaphoreType.DMA((2,)),
        ],
        compiler_params=pltpu.CompilerParams(
            collective_id=0, has_side_effects=True, vmem_limit_bytes=60 << 20
        ),
        cost_estimate=pl.CostEstimate(
            flops=flops, bytes_accessed=8 * wide * units, transcendentals=0
        ),
    )(x, g, s, w1, w2)
    return out[None], gin[None], gw1[None], gw2[None]


def solution(mesh):
    placed = (
        P("peer", "row", "col"),
        P("peer", "col", "row"),
        P("peer", "row", "col"),
        P("peer", "row", "col"),
        P("peer", "row", "col"),
    )
    return jax.shard_map(
        body,
        mesh=mesh,
        in_specs=placed,
        out_specs=(
            P("peer", "row", "col"),
            P("peer", "row", "col"),
            P("peer", "col", "row"),
            P("peer", "row", "col"),
        ),
        check_vma=False,
    )
```

```python
import functools

import jax
import jax.numpy as jnp
from jax import lax
from jax.experimental import pallas as pl
from jax.experimental.pallas import tpu as pltpu
from jax.sharding import PartitionSpec as P

feature_weight = 1.0
SIDE = 4
CHUNKS = 3
CUTS = ((0, 512), (512, 384))
STEPS = 12
ORDER = (
    (0, 0, 1), (0, 0, 0), (1, 0, 1), (0, 1, 1), (1, 0, 0), (0, 1, 0), (1, 1, 0), (1, 1, 1),
    (0, 2, 0), (2, 0, 0), (2, 0, 1), (1, 2, 0), (2, 1, 1), (2, 1, 0), (0, 3, 1), (0, 3, 0),
    (1, 3, 1), (1, 3, 0), (0, 4, 0), (2, 2, 0), (1, 4, 0), (0, 5, 1), (2, 3, 1), (0, 5, 0),
    (1, 5, 0), (0, 6, 1), (0, 6, 0), (2, 3, 0), (1, 5, 1), (0, 7, 1), (0, 7, 0), (2, 4, 0),
    (0, 8, 0), (1, 6, 0), (1, 6, 1), (2, 5, 0), (2, 5, 1), (1, 7, 0), (0, 9, 0), (2, 6, 0),
    (1, 7, 1), (0, 9, 1), (2, 6, 1), (2, 7, 0), (2, 7, 1), (1, 8, 0), (0, 10, 0), (2, 8, 0),
    (1, 9, 0), (1, 9, 1), (0, 13, 0), (0, 11, 1), (0, 11, 0), (2, 9, 0), (2, 9, 1), (1, 10, 0),
    (0, 12, 0), (2, 10, 0), (0, 14, 0), (1, 11, 0), (1, 11, 1), (2, 11, 0), (2, 11, 1), (0, 12, 1),
    (2, 12, 0), (1, 12, 0), (1, 12, 1), (2, 12, 1),
)
MESH = pl.DeviceIdType.MESH
F32 = jnp.float32
BF16 = jnp.bfloat16


def gelu_both(v):
    inner = 0.7978845608 * (v + 0.044715 * v * v * v)
    t = jnp.tanh(inner)
    half = 0.5 * (1.0 + t)
    value = v * half
    slope = half + 0.5 * v * (1.0 - t * t) * (0.7978845608 * (1.0 + 3.0 * 0.044715 * v * v))
    return value, slope


def column_tiles(width, run):
    full = width // 256

    def step(n, carry):
        run(pl.multiple_of(n * 256, 256), 256)
        return carry

    lax.fori_loop(0, full, step, 0)
    if width % 256:
        run(full * 256, width % 256)


def kernel(
    x_ref, g_ref, s_ref, w1_ref, w2_ref,
    out_ref, gin_ref, gw1_ref, gw2_ref,
    w1, w2, stale, x_all, slope_all, hidden_all, inner_all, dgelu,
    part1, part2, got_z1, got_z2, outp, ginp,
    big, small, sum_a, sum_b, gw1, gw2,
    send_sem, recv_sem, stale_sem, local_sem, out_sem,
):
    tokens = x_ref.shape[0] // CHUNKS
    wide, units = w1.shape
    half = wide // 2
    rows = tokens * SIDE * SIDE
    peer, row, z = lax.axis_index("peer"), lax.axis_index("row"), lax.axis_index("col")
    y, x = lax.div(row, SIDE), lax.rem(row, SIDE)

    def at(axis, d):
        if axis == "x":
            return lax.rem(x + d, SIDE)
        if axis == "y":
            return lax.rem(y + d, SIDE)
        return lax.rem(z + d, SIDE)

    def device(axis, d):
        if axis == "x":
            return (peer, y * SIDE + at("x", d), z)
        if axis == "y":
            return (peer, at("y", d) * SIDE + x, z)
        return (peer, row, at("z", d))

    other = (1 - peer, row, z)

    load1 = pltpu.make_async_copy(w1_ref, w1, local_sem.at[0])
    load2 = pltpu.make_async_copy(w2_ref, w2, local_sem.at[1])
    load1.start()
    load2.start()

    barrier = pltpu.get_barrier_semaphore()
    for axis in "xyz":
        for d in range(1, SIDE):
            pl.semaphore_signal(barrier, inc=1, device_id=device(axis, d), device_id_type=MESH)
    pl.semaphore_signal(barrier, inc=1, device_id=other, device_id_type=MESH)
    for k in range(CHUNKS):
        x_all[k, y, x] = x_ref[pl.ds(k * tokens, tokens), :]
    pl.semaphore_wait(barrier, 3 * (SIDE - 1) + 1)

    def send(key, src, dst, target):
        copy = pltpu.make_async_remote_copy(
            src_ref=src,
            dst_ref=dst,
            send_sem=send_sem.at[key],
            recv_sem=recv_sem.at[key],
            device_id=target,
            device_id_type=MESH,
        )
        copy.start()

    def bytes_of(e, g):
        cols = pl.ds(*CUTS[g])
        if e in (2, 3, 8, 9):
            return got_z1.at[0, :, :, cols]
        if e in (0, 5, 6, 11):
            return small.at[0, 0, :, :, :, cols]
        return big.at[0, 0, :, :, :, :, cols]

    def arrive(k, e, g):
        held = bytes_of(e, g)
        pltpu.make_async_copy(held, held, recv_sem.at[k, e, g]).wait()

    def leave(k, e, g):
        held = bytes_of(e, g)
        pltpu.make_async_copy(held, held, send_sem.at[k, e, g]).wait()

    ring = range(1, SIDE)

    def plain(g):
        return pl.ds(*CUTS[g])

    def right(g):
        return pl.ds(half + CUTS[g][0], CUTS[g][1])

    def gather_first(k, e, g, buf):
        a, b = plain(g), right(g)
        for d in ring:
            send((k, e, g), buf.at[k, y, x, :, a], buf.at[k, y, x, :, a], device("x", d))
            send((k, e, g), buf.at[k, y, x, :, b], buf.at[k, y, x, :, b], device("y", d))

    def gather_second(k, e, g, buf):
        arrive(k, e - 1, g)
        a, b = plain(g), right(g)
        for d in ring:
            send((k, e, g), buf.at[k, y, :, :, a], buf.at[k, y, :, :, a], device("y", d))
            send((k, e, g), buf.at[k, :, x, :, b], buf.at[k, :, x, :, b], device("x", d))

    def scatter_first(k, e, g, i, src, weight, flipped, buf):
        a, b = plain(g), right(g)
        to_features(k, src, weight, flipped, buf, a)
        for d in ring:
            there = big.at[i, k, 0, d - 1, :, :, a]
            send((k, e, g), buf.at[k, at("y", d), :, :, a], there, device("y", d))
        to_features(k, src, weight, flipped, buf, b)
        for d in ring:
            there = big.at[i, k, 1, d - 1, :, :, a]
            send((k, e, g), buf.at[k, :, at("x", d), :, b], there, device("x", d))

    def scatter_second(k, e, g, i, buf):
        arrive(k, e - 1, g)
        a, b = plain(g), right(g)
        for n in range(SIDE):
            total = buf[k, y, n, :, a].astype(F32)
            for d in ring:
                total = total + big[i, k, 0, d - 1, n, :, a].astype(F32)
            sum_a[i, k, n, :, a] = total.astype(BF16)
        for d in ring:
            here = sum_a.at[i, k, at("x", d), :, a]
            send((k, e, g), here, small.at[i, k, 0, d - 1, :, a], device("x", d))
        for n in range(SIDE):
            total = buf[k, n, x, :, b].astype(F32)
            for d in ring:
                total = total + big[i, k, 1, d - 1, n, :, a].astype(F32)
            sum_b[i, k, n, :, a] = total.astype(BF16)
        for d in ring:
            here = sum_b.at[i, k, at("y", d), :, a]
            send((k, e, g), here, small.at[i, k, 1, d - 1, :, a], device("y", d))

    def scatter_total(k, e, g, i):
        arrive(k, e - 1, g)
        cols = plain(g)
        a = sum_a[i, k, x, :, cols].astype(F32)
        b = sum_b[i, k, y, :, cols].astype(F32)
        for d in ring:
            a = a + small[i, k, 0, d - 1, :, cols].astype(F32)
            b = b + small[i, k, 1, d - 1, :, cols].astype(F32)
        return (cols, a), (right(g), b)

    def col_scatter(k, e, g, src, weight, flipped, buf, got):
        cols = plain(g)
        to_units(k, src, weight, flipped, buf, cols)
        for d in ring:
            there = got.at[k, d - 1, :, cols]
            send((k, e, g), buf.at[k, at("z", d), :, cols], there, device("z", d))

    def col_total(k, e, g, buf, got):
        arrive(k, e - 1, g)
        cols = plain(g)
        total = buf[k, z, :, cols].astype(F32)
        for d in ring:
            total = total + got[k, d - 1, :, cols].astype(F32)
        return total

    def col_gather(k, e, g, buf):
        here = buf.at[k, z, :, plain(g)]
        for d in ring:
            send((k, e, g), here, here, device("z", d))

    def times(block, weight, flipped, cols):
        if flipped:
            return lax.dot_general(
                block, weight[cols, :], (((1,), (1,)), ((), ())), preferred_element_type=F32
            ).astype(BF16)
        return jnp.dot(block, weight[:, cols], preferred_element_type=F32).astype(BF16)

    def to_units(k, src, weight, flipped, dst, cols):
        value = times(src[k].reshape(rows, wide), weight, flipped, cols)
        dst[k, :, :, cols] = value.reshape(SIDE, rows // SIDE, cols.size)

    def to_features(k, src, weight, flipped, dst, cols):
        value = times(src[k].reshape(rows, units), weight, flipped, cols)
        dst[k, :, :, :, cols] = value.reshape(SIDE, SIDE, tokens, cols.size)

    def local(k):
        return pl.ds(k * tokens, tokens)

    everyone = CHUNKS * rows

    def weight_gradient(narrow, other_all, result, width):
        def tile(start, size):
            a = narrow[..., pl.ds(start, size)].reshape(everyone, size)
            b = other_all[...].reshape(everyone, width)
            result[pl.ds(start, size), :] = lax.dot_general(
                a, b, (((0,), (0,)), ((), ())), preferred_element_type=F32
            ).astype(BF16)

        return tile

    def event(k, e, g):
        groups = range(len(CUTS))
        if e in (2, 4, 8, 10):
            for other_g in groups:
                arrive(k, e - 1, other_g)
        if e == 0:
            gather_first(k, e, g, x_all)
        elif e == 1:
            gather_second(k, e, g, x_all)
        elif e == 2:
            for g in groups:
                col_scatter(k, e, g, x_all, w1, False, part1, got_z1)
        elif e == 3:
            value, slope = gelu_both(col_total(k, e, g, part1, got_z1))
            hidden_all[k, z, :, plain(g)] = value.astype(BF16)
            col_gather(k, e, g, hidden_all)
            dgelu[k, :, plain(g)] = slope
        elif e == 4:
            for g in groups:
                scatter_first(k, e, g, 0, hidden_all, w2, False, outp)
        elif e == 5:
            scatter_second(k, e, g, 0, outp)
        elif e == 6:
            for cols, total in scatter_total(k, e, g, 0):
                output = (x_ref[local(k), cols].astype(F32) + total).astype(BF16)
                out_ref[local(k), cols] = output
                slope = g_ref[local(k), cols].astype(F32) + feature_weight * (
                    output.astype(F32) - stale[local(k), cols].astype(F32)
                )
                slope_all[k, y, x, :, cols] = slope.astype(BF16)
            gather_first(k, e, g, slope_all)
        elif e == 7:
            gather_second(k, e, g, slope_all)
        elif e == 8:
            for g in groups:
                col_scatter(k, e, g, slope_all, w2, True, part2, got_z2)
        elif e == 9:
            inner = col_total(k, e, g, part2, got_z2) * dgelu[k, :, plain(g)]
            inner_all[k, z, :, plain(g)] = inner.astype(BF16)
            col_gather(k, e, g, inner_all)
        elif e == 10:
            for g in groups:
                scatter_first(k, e, g, 1, inner_all, w1, True, ginp)
        elif e == 11:
            scatter_second(k, e, g, 1, ginp)
        elif e == 12:
            for cols, total in scatter_total(k, e, g, 1):
                mine = slope_all[k, y, x, :, cols].astype(F32)
                gin_ref[local(k), cols] = (mine + total).astype(BF16)
        elif e == 13:
            column_tiles(units, weight_gradient(hidden_all, slope_all, gw2, wide))
            save2.start()
        elif e == 14:
            column_tiles(wide, weight_gradient(x_all, inner_all, gw1, units))
            save1.start()

    swap = pltpu.make_async_remote_copy(
        src_ref=s_ref, dst_ref=stale, send_sem=stale_sem.at[0], recv_sem=stale_sem.at[1],
        device_id=other, device_id_type=MESH,
    )
    save1 = pltpu.make_async_copy(gw1, gw1_ref, out_sem.at[0])
    save2 = pltpu.make_async_copy(gw2, gw2_ref, out_sem.at[1])

    once = {1: swap.start, 2: load1.wait, 4: load2.wait, 6: swap.wait_recv}
    for k, e, g in ORDER:
        if e in once:
            once.pop(e)()
        event(k, e, g)
    swap.wait_send()
    for k in range(CHUNKS):
        for e in range(STEPS):
            for g in range(len(CUTS)):
                leave(k, e, g)
    save2.wait()
    save1.wait()


def body(block_in, weight_in, weight_out, upstream, stale_out):
    x, w1, w2, g, s = block_in[0], weight_in[0], weight_out[0], upstream[0], stale_out[0]
    wide, units = w1.shape
    own = x.shape[0]
    tokens = own // CHUNKS
    rows = tokens * SIDE * SIDE
    half = wide // 2
    share = rows // SIDE
    ring = SIDE - 1
    inside = pl.BlockSpec(memory_space=pltpu.VMEM)
    anywhere = pl.BlockSpec(memory_space=pl.ANY)
    row_all = pltpu.VMEM((CHUNKS, SIDE, SIDE, tokens, wide), BF16)
    col_all = pltpu.VMEM((CHUNKS, SIDE, share, units), BF16)
    col_got = pltpu.VMEM((CHUNKS, ring, share, units), BF16)
    flops = 12 * own * 16 * wide * units
    out, gin, gw1, gw2 = pl.pallas_call(
        kernel,
        out_shape=(
            jax.ShapeDtypeStruct(x.shape, BF16),
            jax.ShapeDtypeStruct(x.shape, BF16),
            jax.ShapeDtypeStruct(w1.shape, BF16),
            jax.ShapeDtypeStruct(w2.shape, BF16),
        ),
        in_specs=[inside, inside, inside, anywhere, anywhere],
        out_specs=(inside, inside, anywhere, anywhere),
        scratch_shapes=[
            pltpu.VMEM((wide, units), BF16),
            pltpu.VMEM((units, wide), BF16),
            pltpu.VMEM(x.shape, BF16),
            row_all,
            row_all,
            col_all,
            col_all,
            pltpu.VMEM((CHUNKS, share, units), F32),
            col_all,
            col_all,
            col_got,
            col_got,
            row_all,
            row_all,
            pltpu.VMEM((2, CHUNKS, 2, ring, SIDE, tokens, half), BF16),
            pltpu.VMEM((2, CHUNKS, 2, ring, tokens, half), BF16),
            pltpu.VMEM((2, CHUNKS, SIDE, tokens, half), BF16),
            pltpu.VMEM((2, CHUNKS, SIDE, tokens, half), BF16),
            pltpu.VMEM((wide, units), BF16),
            pltpu.VMEM((units, wide), BF16),
            pltpu.SemaphoreType.DMA((CHUNKS, STEPS, len(CUTS))),
            pltpu.SemaphoreType.DMA((CHUNKS, STEPS, len(CUTS))),
            pltpu.SemaphoreType.DMA((2,)),
            pltpu.SemaphoreType.DMA((2,)),
            pltpu.SemaphoreType.DMA((2,)),
        ],
        compiler_params=pltpu.CompilerParams(
            collective_id=0, has_side_effects=True, vmem_limit_bytes=60 << 20
        ),
        cost_estimate=pl.CostEstimate(
            flops=flops, bytes_accessed=8 * wide * units, transcendentals=0
        ),
    )(x, g, s, w1, w2)
    return out[None], gin[None], gw1[None], gw2[None]


def solution(mesh):
    placed = (
        P("peer", "row", "col"),
        P("peer", "col", "row"),
        P("peer", "row", "col"),
        P("peer", "row", "col"),
        P("peer", "row", "col"),
    )
    return jax.shard_map(
        body,
        mesh=mesh,
        in_specs=placed,
        out_specs=(
            P("peer", "row", "col"),
            P("peer", "row", "col"),
            P("peer", "col", "row"),
            P("peer", "row", "col"),
        ),
        check_vma=False,
    )
```

```python
import functools

import jax
import jax.numpy as jnp
from jax import lax
from jax.experimental import pallas as pl
from jax.experimental.pallas import tpu as pltpu
from jax.sharding import PartitionSpec as P

feature_weight = 1.0
SIDE = 4
CHUNKS = 3
CUTS = ((0, 512), (512, 384))
STEPS = 12
ORDER = (
    (0, 0, 1), (0, 0, 0), (1, 0, 1), (0, 1, 1), (1, 0, 0), (0, 1, 0), (1, 1, 0), (1, 1, 1),
    (0, 2, 0), (2, 0, 0), (2, 0, 1), (1, 2, 0), (2, 1, 1), (2, 1, 0), (0, 3, 1), (0, 3, 0),
    (1, 3, 1), (1, 3, 0), (0, 4, 0), (2, 2, 0), (1, 4, 0), (0, 5, 1), (2, 3, 1), (0, 5, 0),
    (1, 5, 0), (0, 6, 1), (0, 6, 0), (2, 3, 0), (1, 5, 1), (0, 7, 1), (0, 7, 0), (2, 4, 0),
    (0, 8, 0), (1, 6, 0), (1, 6, 1), (2, 5, 0), (2, 5, 1), (1, 7, 0), (0, 9, 0), (2, 6, 0),
    (1, 7, 1), (0, 9, 1), (2, 6, 1), (2, 7, 0), (2, 7, 1), (1, 8, 0), (0, 10, 0), (2, 8, 0),
    (1, 9, 0), (1, 9, 1), (0, 13, 0), (0, 11, 1), (0, 11, 0), (2, 9, 0), (2, 9, 1), (1, 10, 0),
    (0, 12, 0), (2, 10, 0), (0, 14, 0), (1, 11, 0), (1, 11, 1), (2, 11, 0), (2, 11, 1), (0, 12, 1),
    (2, 12, 0), (1, 12, 0), (1, 12, 1), (2, 12, 1),
)
MESH = pl.DeviceIdType.MESH
F32 = jnp.float32
BF16 = jnp.bfloat16


def gelu_both(v):
    inner = 0.7978845608 * (v + 0.044715 * v * v * v)
    t = jnp.tanh(inner)
    half = 0.5 * (1.0 + t)
    value = v * half
    slope = half + 0.5 * v * (1.0 - t * t) * (0.7978845608 * (1.0 + 3.0 * 0.044715 * v * v))
    return value, slope


def column_tiles(width, run):
    full = width // 256

    def step(n, carry):
        run(pl.multiple_of(n * 256, 256), 256)
        return carry

    lax.fori_loop(0, full, step, 0)
    if width % 256:
        run(full * 256, width % 256)


def kernel(
    x_ref, g_ref, s_ref, w1_ref, w2_ref,
    out_ref, gin_ref, gw1_ref, gw2_ref,
    w1, w2, stale, x_all, slope_all, hidden_all, inner_all, dgelu,
    part1, part2, got_z1, got_z2, outp, ginp,
    big, small, sum_a, sum_b,
    send_sem, recv_sem, stale_sem, local_sem,
):
    tokens = x_ref.shape[0] // CHUNKS
    wide, units = w1.shape
    half = wide // 2
    rows = tokens * SIDE * SIDE
    peer, row, z = lax.axis_index("peer"), lax.axis_index("row"), lax.axis_index("col")
    y, x = lax.div(row, SIDE), lax.rem(row, SIDE)

    def at(axis, d):
        if axis == "x":
            return lax.rem(x + d, SIDE)
        if axis == "y":
            return lax.rem(y + d, SIDE)
        return lax.rem(z + d, SIDE)

    def device(axis, d):
        if axis == "x":
            return (peer, y * SIDE + at("x", d), z)
        if axis == "y":
            return (peer, at("y", d) * SIDE + x, z)
        return (peer, row, at("z", d))

    other = (1 - peer, row, z)

    load1 = pltpu.make_async_copy(w1_ref, w1, local_sem.at[0])
    load2 = pltpu.make_async_copy(w2_ref, w2, local_sem.at[1])
    load1.start()
    load2.start()

    barrier = pltpu.get_barrier_semaphore()
    for axis in "xyz":
        for d in range(1, SIDE):
            pl.semaphore_signal(barrier, inc=1, device_id=device(axis, d), device_id_type=MESH)
    pl.semaphore_signal(barrier, inc=1, device_id=other, device_id_type=MESH)
    for k in range(CHUNKS):
        x_all[k, y, x] = x_ref[pl.ds(k * tokens, tokens), :]
    pl.semaphore_wait(barrier, 3 * (SIDE - 1) + 1)

    def send(key, src, dst, target):
        copy = pltpu.make_async_remote_copy(
            src_ref=src,
            dst_ref=dst,
            send_sem=send_sem.at[key],
            recv_sem=recv_sem.at[key],
            device_id=target,
            device_id_type=MESH,
        )
        copy.start()

    def bytes_of(e, g):
        cols = pl.ds(*CUTS[g])
        if e in (2, 3, 8, 9):
            return got_z1.at[0, :, :, cols]
        if e in (0, 5, 6, 11):
            return small.at[0, 0, :, :, :, cols]
        return big.at[0, 0, :, :, :, :, cols]

    def arrive(k, e, g):
        held = bytes_of(e, g)
        pltpu.make_async_copy(held, held, recv_sem.at[k, e, g]).wait()

    def leave(k, e, g):
        held = bytes_of(e, g)
        pltpu.make_async_copy(held, held, send_sem.at[k, e, g]).wait()

    ring = range(1, SIDE)

    def plain(g):
        return pl.ds(*CUTS[g])

    def right(g):
        return pl.ds(half + CUTS[g][0], CUTS[g][1])

    def gather_first(k, e, g, buf):
        a, b = plain(g), right(g)
        for d in ring:
            send((k, e, g), buf.at[k, y, x, :, a], buf.at[k, y, x, :, a], device("x", d))
            send((k, e, g), buf.at[k, y, x, :, b], buf.at[k, y, x, :, b], device("y", d))

    def gather_second(k, e, g, buf):
        arrive(k, e - 1, g)
        a, b = plain(g), right(g)
        for d in ring:
            send((k, e, g), buf.at[k, y, :, :, a], buf.at[k, y, :, :, a], device("y", d))
            send((k, e, g), buf.at[k, :, x, :, b], buf.at[k, :, x, :, b], device("x", d))

    def scatter_first(k, e, g, i, src, weight, flipped, buf):
        a, b = plain(g), right(g)
        to_features(k, src, weight, flipped, buf, a)
        for d in ring:
            there = big.at[i, k, 0, d - 1, :, :, a]
            send((k, e, g), buf.at[k, at("y", d), :, :, a], there, device("y", d))
        to_features(k, src, weight, flipped, buf, b)
        for d in ring:
            there = big.at[i, k, 1, d - 1, :, :, a]
            send((k, e, g), buf.at[k, :, at("x", d), :, b], there, device("x", d))

    def scatter_second(k, e, g, i, buf):
        arrive(k, e - 1, g)
        a, b = plain(g), right(g)
        for n in range(SIDE):
            total = buf[k, y, n, :, a].astype(F32)
            for d in ring:
                total = total + big[i, k, 0, d - 1, n, :, a].astype(F32)
            sum_a[i, k, n, :, a] = total.astype(BF16)
        for d in ring:
            here = sum_a.at[i, k, at("x", d), :, a]
            send((k, e, g), here, small.at[i, k, 0, d - 1, :, a], device("x", d))
        for n in range(SIDE):
            total = buf[k, n, x, :, b].astype(F32)
            for d in ring:
                total = total + big[i, k, 1, d - 1, n, :, a].astype(F32)
            sum_b[i, k, n, :, a] = total.astype(BF16)
        for d in ring:
            here = sum_b.at[i, k, at("y", d), :, a]
            send((k, e, g), here, small.at[i, k, 1, d - 1, :, a], device("y", d))

    def scatter_total(k, e, g, i):
        arrive(k, e - 1, g)
        cols = plain(g)
        a = sum_a[i, k, x, :, cols].astype(F32)
        b = sum_b[i, k, y, :, cols].astype(F32)
        for d in ring:
            a = a + small[i, k, 0, d - 1, :, cols].astype(F32)
            b = b + small[i, k, 1, d - 1, :, cols].astype(F32)
        return (cols, a), (right(g), b)

    def col_scatter(k, e, g, src, weight, flipped, buf, got):
        cols = plain(g)
        to_units(k, src, weight, flipped, buf, cols)
        for d in ring:
            there = got.at[k, d - 1, :, cols]
            send((k, e, g), buf.at[k, at("z", d), :, cols], there, device("z", d))

    def col_total(k, e, g, buf, got):
        arrive(k, e - 1, g)
        cols = plain(g)
        total = buf[k, z, :, cols].astype(F32)
        for d in ring:
            total = total + got[k, d - 1, :, cols].astype(F32)
        return total

    def col_gather(k, e, g, buf):
        here = buf.at[k, z, :, plain(g)]
        for d in ring:
            send((k, e, g), here, here, device("z", d))

    def times(block, weight, flipped, cols):
        if flipped:
            return lax.dot_general(
                block, weight[cols, :], (((1,), (1,)), ((), ())), preferred_element_type=F32
            ).astype(BF16)
        return jnp.dot(block, weight[:, cols], preferred_element_type=F32).astype(BF16)

    def to_units(k, src, weight, flipped, dst, cols):
        value = times(src[k].reshape(rows, wide), weight, flipped, cols)
        dst[k, :, :, cols] = value.reshape(SIDE, rows // SIDE, cols.size)

    def to_features(k, src, weight, flipped, dst, cols):
        value = times(src[k].reshape(rows, units), weight, flipped, cols)
        dst[k, :, :, :, cols] = value.reshape(SIDE, SIDE, tokens, cols.size)

    def local(k):
        return pl.ds(k * tokens, tokens)

    everyone = CHUNKS * rows

    def weight_gradient(narrow, other_all, result, width):
        def tile(start, size):
            a = narrow[..., pl.ds(start, size)].reshape(everyone, size)
            b = other_all[...].reshape(everyone, width)
            result[pl.ds(start, size), :] = lax.dot_general(
                a, b, (((0,), (0,)), ((), ())), preferred_element_type=F32
            ).astype(BF16)

        return tile

    def event(k, e, g):
        groups = range(len(CUTS))
        if e in (2, 4, 8, 10):
            for other_g in groups:
                arrive(k, e - 1, other_g)
        if e == 0:
            gather_first(k, e, g, x_all)
        elif e == 1:
            gather_second(k, e, g, x_all)
        elif e == 2:
            for g in groups:
                col_scatter(k, e, g, x_all, w1, False, part1, got_z1)
        elif e == 3:
            value, slope = gelu_both(col_total(k, e, g, part1, got_z1))
            hidden_all[k, z, :, plain(g)] = value.astype(BF16)
            col_gather(k, e, g, hidden_all)
            dgelu[k, :, plain(g)] = slope
        elif e == 4:
            for g in groups:
                scatter_first(k, e, g, 0, hidden_all, w2, False, outp)
        elif e == 5:
            scatter_second(k, e, g, 0, outp)
        elif e == 6:
            for cols, total in scatter_total(k, e, g, 0):
                output = (x_ref[local(k), cols].astype(F32) + total).astype(BF16)
                out_ref[local(k), cols] = output
                slope = g_ref[local(k), cols].astype(F32) + feature_weight * (
                    output.astype(F32) - stale[local(k), cols].astype(F32)
                )
                slope_all[k, y, x, :, cols] = slope.astype(BF16)
            gather_first(k, e, g, slope_all)
        elif e == 7:
            gather_second(k, e, g, slope_all)
        elif e == 8:
            for g in groups:
                col_scatter(k, e, g, slope_all, w2, True, part2, got_z2)
        elif e == 9:
            inner = col_total(k, e, g, part2, got_z2) * dgelu[k, :, plain(g)]
            inner_all[k, z, :, plain(g)] = inner.astype(BF16)
            col_gather(k, e, g, inner_all)
        elif e == 10:
            for g in groups:
                scatter_first(k, e, g, 1, inner_all, w1, True, ginp)
        elif e == 11:
            scatter_second(k, e, g, 1, ginp)
        elif e == 12:
            for cols, total in scatter_total(k, e, g, 1):
                mine = slope_all[k, y, x, :, cols].astype(F32)
                gin_ref[local(k), cols] = (mine + total).astype(BF16)
        elif e == 13:
            column_tiles(units, weight_gradient(hidden_all, slope_all, gw2_ref, wide))
        elif e == 14:
            column_tiles(wide, weight_gradient(x_all, inner_all, gw1_ref, units))

    swap = pltpu.make_async_remote_copy(
        src_ref=s_ref, dst_ref=stale, send_sem=stale_sem.at[0], recv_sem=stale_sem.at[1],
        device_id=other, device_id_type=MESH,
    )
    once = {1: swap.start, 2: load1.wait, 4: load2.wait, 6: swap.wait_recv}
    for k, e, g in ORDER:
        if e in once:
            once.pop(e)()
        event(k, e, g)
    swap.wait_send()
    for k in range(CHUNKS):
        for e in range(STEPS):
            for g in range(len(CUTS)):
                leave(k, e, g)


def body(block_in, weight_in, weight_out, upstream, stale_out):
    x, w1, w2, g, s = block_in[0], weight_in[0], weight_out[0], upstream[0], stale_out[0]
    wide, units = w1.shape
    own = x.shape[0]
    tokens = own // CHUNKS
    rows = tokens * SIDE * SIDE
    half = wide // 2
    share = rows // SIDE
    ring = SIDE - 1
    inside = pl.BlockSpec(memory_space=pltpu.VMEM)
    anywhere = pl.BlockSpec(memory_space=pl.ANY)
    row_all = pltpu.VMEM((CHUNKS, SIDE, SIDE, tokens, wide), BF16)
    col_all = pltpu.VMEM((CHUNKS, SIDE, share, units), BF16)
    col_got = pltpu.VMEM((CHUNKS, ring, share, units), BF16)
    flops = 12 * own * 16 * wide * units
    out, gin, gw1, gw2 = pl.pallas_call(
        kernel,
        out_shape=(
            jax.ShapeDtypeStruct(x.shape, BF16),
            jax.ShapeDtypeStruct(x.shape, BF16),
            jax.ShapeDtypeStruct(w1.shape, BF16),
            jax.ShapeDtypeStruct(w2.shape, BF16),
        ),
        in_specs=[inside, inside, inside, anywhere, anywhere],
        out_specs=(inside,) * 4,
        scratch_shapes=[
            pltpu.VMEM((wide, units), BF16),
            pltpu.VMEM((units, wide), BF16),
            pltpu.VMEM(x.shape, BF16),
            row_all,
            row_all,
            col_all,
            col_all,
            pltpu.VMEM((CHUNKS, share, units), F32),
            col_all,
            col_all,
            col_got,
            col_got,
            row_all,
            row_all,
            pltpu.VMEM((2, CHUNKS, 2, ring, SIDE, tokens, half), BF16),
            pltpu.VMEM((2, CHUNKS, 2, ring, tokens, half), BF16),
            pltpu.VMEM((2, CHUNKS, SIDE, tokens, half), BF16),
            pltpu.VMEM((2, CHUNKS, SIDE, tokens, half), BF16),
            pltpu.SemaphoreType.DMA((CHUNKS, STEPS, len(CUTS))),
            pltpu.SemaphoreType.DMA((CHUNKS, STEPS, len(CUTS))),
            pltpu.SemaphoreType.DMA((2,)),
            pltpu.SemaphoreType.DMA((2,)),
        ],
        compiler_params=pltpu.CompilerParams(
            collective_id=0, has_side_effects=True, vmem_limit_bytes=44 << 20
        ),
        cost_estimate=pl.CostEstimate(
            flops=flops, bytes_accessed=8 * wide * units, transcendentals=0
        ),
    )(x, g, s, w1, w2)
    return out[None], gin[None], gw1[None], gw2[None]


def solution(mesh):
    placed = (
        P("peer", "row", "col"),
        P("peer", "col", "row"),
        P("peer", "row", "col"),
        P("peer", "row", "col"),
        P("peer", "row", "col"),
    )
    return jax.shard_map(
        body,
        mesh=mesh,
        in_specs=placed,
        out_specs=(
            P("peer", "row", "col"),
            P("peer", "row", "col"),
            P("peer", "col", "row"),
            P("peer", "row", "col"),
        ),
        check_vma=False,
    )
```

```python
import functools

import jax
import jax.numpy as jnp
from jax import lax
from jax.experimental import pallas as pl
from jax.experimental.pallas import tpu as pltpu
from jax.sharding import PartitionSpec as P

feature_weight = 1.0
SIDE = 4
CHUNKS = 3
CUTS = ((0, 512), (512, 384))
STEPS = 12
ORDER = (
    (0, 0, 1), (1, 0, 0), (1, 0, 1), (0, 0, 0), (2, 0, 0), (0, 1, 1), (0, 1, 0), (0, 2, 0),
    (2, 0, 1), (1, 1, 1), (2, 1, 0), (1, 1, 0), (0, 3, 0), (0, 3, 1), (1, 2, 0), (2, 1, 1),
    (0, 4, 0), (1, 3, 0), (1, 3, 1), (0, 5, 0), (2, 2, 0), (0, 5, 1), (0, 6, 0), (1, 4, 0),
    (0, 6, 1), (2, 3, 0), (0, 7, 0), (2, 3, 1), (0, 7, 1), (1, 5, 0), (1, 5, 1), (2, 4, 0),
    (0, 8, 0), (1, 6, 0), (2, 5, 0), (1, 6, 1), (1, 7, 0), (2, 5, 1), (0, 9, 1), (2, 6, 0),
    (0, 9, 0), (1, 7, 1), (2, 6, 1), (2, 7, 0), (2, 7, 1), (1, 8, 0), (0, 10, 0), (2, 8, 0),
    (0, 11, 0), (1, 9, 0), (1, 9, 1), (0, 13, 1), (0, 13, 0), (0, 11, 1), (2, 9, 1), (2, 9, 0),
    (1, 10, 0), (2, 10, 0), (0, 14, 1), (0, 14, 0), (1, 11, 1), (0, 14, 2), (1, 11, 0), (2, 11, 0),
    (2, 11, 1), (1, 12, 1), (0, 12, 0), (0, 14, 3), (2, 12, 0), (1, 12, 0), (0, 12, 1), (2, 12, 1),
)
MESH = pl.DeviceIdType.MESH
F32 = jnp.float32
BF16 = jnp.bfloat16


def gelu_both(v):
    inner = 0.7978845608 * (v + 0.044715 * v * v * v)
    t = jnp.tanh(inner)
    half = 0.5 * (1.0 + t)
    value = v * half
    slope = half + 0.5 * v * (1.0 - t * t) * (0.7978845608 * (1.0 + 3.0 * 0.044715 * v * v))
    return value, slope


def column_tiles(part, width, run):
    for start in range(part * 512, min(width, part * 512 + 512), 256):
        run(start, min(256, width - start))


def kernel(
    x_ref, g_ref, s_ref, w1_ref, w2_ref,
    out_ref, gin_ref, gw1_ref, gw2_ref,
    w1, w2, stale, x_all, slope_all, hidden_all, inner_all, dgelu,
    part1, part2, got_z1, got_z2, outp, ginp,
    big, small, sum_a, sum_b,
    send_sem, recv_sem, stale_sem, local_sem,
):
    tokens = x_ref.shape[0] // CHUNKS
    wide, units = w1.shape
    half = wide // 2
    rows = tokens * SIDE * SIDE
    peer, row, z = lax.axis_index("peer"), lax.axis_index("row"), lax.axis_index("col")
    y, x = lax.div(row, SIDE), lax.rem(row, SIDE)

    def at(axis, d):
        if axis == "x":
            return lax.rem(x + d, SIDE)
        if axis == "y":
            return lax.rem(y + d, SIDE)
        return lax.rem(z + d, SIDE)

    def device(axis, d):
        if axis == "x":
            return (peer, y * SIDE + at("x", d), z)
        if axis == "y":
            return (peer, at("y", d) * SIDE + x, z)
        return (peer, row, at("z", d))

    other = (1 - peer, row, z)

    load1 = pltpu.make_async_copy(w1_ref, w1, local_sem.at[0])
    load2 = pltpu.make_async_copy(w2_ref, w2, local_sem.at[1])
    load1.start()
    load2.start()

    barrier = pltpu.get_barrier_semaphore()
    for axis in "xyz":
        for d in range(1, SIDE):
            pl.semaphore_signal(barrier, inc=1, device_id=device(axis, d), device_id_type=MESH)
    pl.semaphore_signal(barrier, inc=1, device_id=other, device_id_type=MESH)
    for k in range(CHUNKS):
        x_all[k, y, x] = x_ref[pl.ds(k * tokens, tokens), :]
    pl.semaphore_wait(barrier, 3 * (SIDE - 1) + 1)

    def send(key, src, dst, target):
        copy = pltpu.make_async_remote_copy(
            src_ref=src,
            dst_ref=dst,
            send_sem=send_sem.at[key],
            recv_sem=recv_sem.at[key],
            device_id=target,
            device_id_type=MESH,
        )
        copy.start()

    def bytes_of(e, g):
        cols = pl.ds(*CUTS[g])
        if e in (2, 3, 8, 9):
            return got_z1.at[0, :, :, cols]
        if e in (0, 5, 6, 11):
            return small.at[0, 0, :, :, :, cols]
        return big.at[0, 0, :, :, :, :, cols]

    def arrive(k, e, g):
        held = bytes_of(e, g)
        pltpu.make_async_copy(held, held, recv_sem.at[k, e, g]).wait()

    def leave(k, e, g):
        held = bytes_of(e, g)
        pltpu.make_async_copy(held, held, send_sem.at[k, e, g]).wait()

    ring = range(1, SIDE)

    def plain(g):
        return pl.ds(*CUTS[g])

    def right(g):
        return pl.ds(half + CUTS[g][0], CUTS[g][1])

    def gather_first(k, e, g, buf):
        a, b = plain(g), right(g)
        for d in ring:
            send((k, e, g), buf.at[k, y, x, :, a], buf.at[k, y, x, :, a], device("x", d))
            send((k, e, g), buf.at[k, y, x, :, b], buf.at[k, y, x, :, b], device("y", d))

    def gather_second(k, e, g, buf):
        arrive(k, e - 1, g)
        a, b = plain(g), right(g)
        for d in ring:
            send((k, e, g), buf.at[k, y, :, :, a], buf.at[k, y, :, :, a], device("y", d))
            send((k, e, g), buf.at[k, :, x, :, b], buf.at[k, :, x, :, b], device("x", d))

    def scatter_first(k, e, g, i, src, weight, flipped, buf):
        a, b = plain(g), right(g)
        to_features(k, src, weight, flipped, buf, a)
        for d in ring:
            there = big.at[i, k, 0, d - 1, :, :, a]
            send((k, e, g), buf.at[k, at("y", d), :, :, a], there, device("y", d))
        to_features(k, src, weight, flipped, buf, b)
        for d in ring:
            there = big.at[i, k, 1, d - 1, :, :, a]
            send((k, e, g), buf.at[k, :, at("x", d), :, b], there, device("x", d))

    def scatter_second(k, e, g, i, buf):
        arrive(k, e - 1, g)
        a, b = plain(g), right(g)
        for n in range(SIDE):
            total = buf[k, y, n, :, a].astype(F32)
            for d in ring:
                total = total + big[i, k, 0, d - 1, n, :, a].astype(F32)
            sum_a[i, k, n, :, a] = total.astype(BF16)
        for d in ring:
            here = sum_a.at[i, k, at("x", d), :, a]
            send((k, e, g), here, small.at[i, k, 0, d - 1, :, a], device("x", d))
        for n in range(SIDE):
            total = buf[k, n, x, :, b].astype(F32)
            for d in ring:
                total = total + big[i, k, 1, d - 1, n, :, a].astype(F32)
            sum_b[i, k, n, :, a] = total.astype(BF16)
        for d in ring:
            here = sum_b.at[i, k, at("y", d), :, a]
            send((k, e, g), here, small.at[i, k, 1, d - 1, :, a], device("y", d))

    def scatter_total(k, e, g, i):
        arrive(k, e - 1, g)
        cols = plain(g)
        a = sum_a[i, k, x, :, cols].astype(F32)
        b = sum_b[i, k, y, :, cols].astype(F32)
        for d in ring:
            a = a + small[i, k, 0, d - 1, :, cols].astype(F32)
            b = b + small[i, k, 1, d - 1, :, cols].astype(F32)
        return (cols, a), (right(g), b)

    def col_scatter(k, e, g, src, weight, flipped, buf, got):
        cols = plain(g)
        to_units(k, src, weight, flipped, buf, cols)
        for d in ring:
            there = got.at[k, d - 1, :, cols]
            send((k, e, g), buf.at[k, at("z", d), :, cols], there, device("z", d))

    def col_total(k, e, g, buf, got):
        arrive(k, e - 1, g)
        cols = plain(g)
        total = buf[k, z, :, cols].astype(F32)
        for d in ring:
            total = total + got[k, d - 1, :, cols].astype(F32)
        return total

    def col_gather(k, e, g, buf):
        here = buf.at[k, z, :, plain(g)]
        for d in ring:
            send((k, e, g), here, here, device("z", d))

    def times(block, weight, flipped, cols):
        if flipped:
            return lax.dot_general(
                block, weight[cols, :], (((1,), (1,)), ((), ())), preferred_element_type=F32
            ).astype(BF16)
        return jnp.dot(block, weight[:, cols], preferred_element_type=F32).astype(BF16)

    def to_units(k, src, weight, flipped, dst, cols):
        value = times(src[k].reshape(rows, wide), weight, flipped, cols)
        dst[k, :, :, cols] = value.reshape(SIDE, rows // SIDE, cols.size)

    def to_features(k, src, weight, flipped, dst, cols):
        value = times(src[k].reshape(rows, units), weight, flipped, cols)
        dst[k, :, :, :, cols] = value.reshape(SIDE, SIDE, tokens, cols.size)

    def local(k):
        return pl.ds(k * tokens, tokens)

    everyone = CHUNKS * rows

    def weight_gradient(narrow, other_all, result, width):
        def tile(start, size):
            a = narrow[..., pl.ds(start, size)].reshape(everyone, size)
            b = other_all[...].reshape(everyone, width)
            result[pl.ds(start, size), :] = lax.dot_general(
                a, b, (((0,), (0,)), ((), ())), preferred_element_type=F32
            ).astype(BF16)

        return tile

    def event(k, e, g):
        groups = range(len(CUTS))
        if e in (2, 4, 8, 10):
            for other_g in groups:
                arrive(k, e - 1, other_g)
        if e == 0:
            gather_first(k, e, g, x_all)
        elif e == 1:
            gather_second(k, e, g, x_all)
        elif e == 2:
            for g in groups:
                col_scatter(k, e, g, x_all, w1, False, part1, got_z1)
        elif e == 3:
            value, slope = gelu_both(col_total(k, e, g, part1, got_z1))
            hidden_all[k, z, :, plain(g)] = value.astype(BF16)
            col_gather(k, e, g, hidden_all)
            dgelu[k, :, plain(g)] = slope
        elif e == 4:
            for g in groups:
                scatter_first(k, e, g, 0, hidden_all, w2, False, outp)
        elif e == 5:
            scatter_second(k, e, g, 0, outp)
        elif e == 6:
            for cols, total in scatter_total(k, e, g, 0):
                output = (x_ref[local(k), cols].astype(F32) + total).astype(BF16)
                out_ref[local(k), cols] = output
                slope = g_ref[local(k), cols].astype(F32) + feature_weight * (
                    output.astype(F32) - stale[local(k), cols].astype(F32)
                )
                slope_all[k, y, x, :, cols] = slope.astype(BF16)
            gather_first(k, e, g, slope_all)
        elif e == 7:
            gather_second(k, e, g, slope_all)
        elif e == 8:
            for g in groups:
                col_scatter(k, e, g, slope_all, w2, True, part2, got_z2)
        elif e == 9:
            inner = col_total(k, e, g, part2, got_z2) * dgelu[k, :, plain(g)]
            inner_all[k, z, :, plain(g)] = inner.astype(BF16)
            col_gather(k, e, g, inner_all)
        elif e == 10:
            for g in groups:
                scatter_first(k, e, g, 1, inner_all, w1, True, ginp)
        elif e == 11:
            scatter_second(k, e, g, 1, ginp)
        elif e == 12:
            for cols, total in scatter_total(k, e, g, 1):
                mine = slope_all[k, y, x, :, cols].astype(F32)
                gin_ref[local(k), cols] = (mine + total).astype(BF16)
        elif e == 13:
            column_tiles(g, units, weight_gradient(hidden_all, slope_all, gw2_ref, wide))
        elif e == 14:
            column_tiles(g, wide, weight_gradient(x_all, inner_all, gw1_ref, units))

    swap = pltpu.make_async_remote_copy(
        src_ref=s_ref, dst_ref=stale, send_sem=stale_sem.at[0], recv_sem=stale_sem.at[1],
        device_id=other, device_id_type=MESH,
    )
    once = {1: swap.start, 2: load1.wait, 4: load2.wait, 6: swap.wait_recv}
    for k, e, g in ORDER:
        if e in once:
            once.pop(e)()
        event(k, e, g)
    swap.wait_send()
    for k in range(CHUNKS):
        for e in range(STEPS):
            for g in range(len(CUTS)):
                leave(k, e, g)


def body(block_in, weight_in, weight_out, upstream, stale_out):
    x, w1, w2, g, s = block_in[0], weight_in[0], weight_out[0], upstream[0], stale_out[0]
    wide, units = w1.shape
    own = x.shape[0]
    tokens = own // CHUNKS
    rows = tokens * SIDE * SIDE
    half = wide // 2
    share = rows // SIDE
    ring = SIDE - 1
    inside = pl.BlockSpec(memory_space=pltpu.VMEM)
    anywhere = pl.BlockSpec(memory_space=pl.ANY)
    row_all = pltpu.VMEM((CHUNKS, SIDE, SIDE, tokens, wide), BF16)
    col_all = pltpu.VMEM((CHUNKS, SIDE, share, units), BF16)
    col_got = pltpu.VMEM((CHUNKS, ring, share, units), BF16)
    flops = 12 * own * 16 * wide * units
    out, gin, gw1, gw2 = pl.pallas_call(
        kernel,
        out_shape=(
            jax.ShapeDtypeStruct(x.shape, BF16),
            jax.ShapeDtypeStruct(x.shape, BF16),
            jax.ShapeDtypeStruct(w1.shape, BF16),
            jax.ShapeDtypeStruct(w2.shape, BF16),
        ),
        in_specs=[inside, inside, inside, anywhere, anywhere],
        out_specs=(inside,) * 4,
        scratch_shapes=[
            pltpu.VMEM((wide, units), BF16),
            pltpu.VMEM((units, wide), BF16),
            pltpu.VMEM(x.shape, BF16),
            row_all,
            row_all,
            col_all,
            col_all,
            pltpu.VMEM((CHUNKS, share, units), F32),
            col_all,
            col_all,
            col_got,
            col_got,
            row_all,
            row_all,
            pltpu.VMEM((2, CHUNKS, 2, ring, SIDE, tokens, half), BF16),
            pltpu.VMEM((2, CHUNKS, 2, ring, tokens, half), BF16),
            pltpu.VMEM((2, CHUNKS, SIDE, tokens, half), BF16),
            pltpu.VMEM((2, CHUNKS, SIDE, tokens, half), BF16),
            pltpu.SemaphoreType.DMA((CHUNKS, STEPS, len(CUTS))),
            pltpu.SemaphoreType.DMA((CHUNKS, STEPS, len(CUTS))),
            pltpu.SemaphoreType.DMA((2,)),
            pltpu.SemaphoreType.DMA((2,)),
        ],
        compiler_params=pltpu.CompilerParams(
            collective_id=0, has_side_effects=True, vmem_limit_bytes=44 << 20
        ),
        cost_estimate=pl.CostEstimate(
            flops=flops, bytes_accessed=8 * wide * units, transcendentals=0
        ),
    )(x, g, s, w1, w2)
    return out[None], gin[None], gw1[None], gw2[None]


def solution(mesh):
    placed = (
        P("peer", "row", "col"),
        P("peer", "col", "row"),
        P("peer", "row", "col"),
        P("peer", "row", "col"),
        P("peer", "row", "col"),
    )
    return jax.shard_map(
        body,
        mesh=mesh,
        in_specs=placed,
        out_specs=(
            P("peer", "row", "col"),
            P("peer", "row", "col"),
            P("peer", "col", "row"),
            P("peer", "row", "col"),
        ),
        check_vma=False,
    )
```

```python
import functools

import jax
import jax.numpy as jnp
from jax import lax
from jax.experimental import pallas as pl
from jax.experimental.pallas import tpu as pltpu
from jax.sharding import PartitionSpec as P

feature_weight = 1.0
SIDE = 4
CHUNKS = 3
CUTS = ((0, 384), (384, 512))
STEPS = 12
ORDER = (
    (0, 0, 1), (1, 0, 0), (1, 0, 1), (0, 0, 0), (2, 0, 0), (0, 1, 1), (0, 1, 0), (0, 2, 0),
    (2, 0, 1), (1, 1, 1), (2, 1, 0), (1, 1, 0), (0, 3, 0), (0, 3, 1), (1, 2, 0), (2, 1, 1),
    (0, 4, 0), (1, 3, 0), (1, 3, 1), (0, 5, 0), (2, 2, 0), (0, 5, 1), (0, 6, 0), (1, 4, 0),
    (0, 6, 1), (2, 3, 0), (0, 7, 0), (2, 3, 1), (0, 7, 1), (1, 5, 0), (1, 5, 1), (2, 4, 0),
    (0, 8, 0), (1, 6, 0), (2, 5, 0), (1, 6, 1), (1, 7, 0), (2, 5, 1), (0, 9, 1), (2, 6, 0),
    (0, 9, 0), (1, 7, 1), (2, 6, 1), (2, 7, 0), (2, 7, 1), (1, 8, 0), (0, 10, 0), (2, 8, 0),
    (0, 11, 0), (1, 9, 0), (1, 9, 1), (0, 13, 1), (0, 13, 0), (0, 11, 1), (2, 9, 1), (2, 9, 0),
    (1, 10, 0), (2, 10, 0), (0, 14, 1), (0, 14, 0), (1, 11, 1), (0, 14, 2), (1, 11, 0), (2, 11, 0),
    (2, 11, 1), (1, 12, 1), (0, 12, 0), (0, 14, 3), (2, 12, 0), (1, 12, 0), (0, 12, 1), (2, 12, 1),
)
MESH = pl.DeviceIdType.MESH
F32 = jnp.float32
BF16 = jnp.bfloat16


def gelu_both(v):
    inner = 0.7978845608 * (v + 0.044715 * v * v * v)
    t = jnp.tanh(inner)
    half = 0.5 * (1.0 + t)
    value = v * half
    slope = half + 0.5 * v * (1.0 - t * t) * (0.7978845608 * (1.0 + 3.0 * 0.044715 * v * v))
    return value, slope


def column_tiles(part, width, run):
    for start in range(part * 512, min(width, part * 512 + 512), 256):
        run(start, min(256, width - start))


def kernel(
    x_ref, g_ref, s_ref, w1_ref, w2_ref,
    out_ref, gin_ref, gw1_ref, gw2_ref,
    w1, w2, stale, x_all, slope_all, hidden_all, inner_all, dgelu,
    part1, part2, got_z1, got_z2, outp, ginp,
    big, small, sum_a, sum_b,
    send_sem, recv_sem, stale_sem, local_sem,
):
    tokens = x_ref.shape[0] // CHUNKS
    wide, units = w1.shape
    half = wide // 2
    rows = tokens * SIDE * SIDE
    peer, row, z = lax.axis_index("peer"), lax.axis_index("row"), lax.axis_index("col")
    y, x = lax.div(row, SIDE), lax.rem(row, SIDE)

    def at(axis, d):
        if axis == "x":
            return lax.rem(x + d, SIDE)
        if axis == "y":
            return lax.rem(y + d, SIDE)
        return lax.rem(z + d, SIDE)

    def device(axis, d):
        if axis == "x":
            return (peer, y * SIDE + at("x", d), z)
        if axis == "y":
            return (peer, at("y", d) * SIDE + x, z)
        return (peer, row, at("z", d))

    other = (1 - peer, row, z)

    load1 = pltpu.make_async_copy(w1_ref, w1, local_sem.at[0])
    load2 = pltpu.make_async_copy(w2_ref, w2, local_sem.at[1])
    load1.start()
    load2.start()

    barrier = pltpu.get_barrier_semaphore()
    for axis in "xyz":
        for d in range(1, SIDE):
            pl.semaphore_signal(barrier, inc=1, device_id=device(axis, d), device_id_type=MESH)
    pl.semaphore_signal(barrier, inc=1, device_id=other, device_id_type=MESH)
    for k in range(CHUNKS):
        x_all[k, y, x] = x_ref[pl.ds(k * tokens, tokens), :]
    pl.semaphore_wait(barrier, 3 * (SIDE - 1) + 1)

    def send(key, src, dst, target):
        copy = pltpu.make_async_remote_copy(
            src_ref=src,
            dst_ref=dst,
            send_sem=send_sem.at[key],
            recv_sem=recv_sem.at[key],
            device_id=target,
            device_id_type=MESH,
        )
        copy.start()

    def bytes_of(e, g):
        cols = pl.ds(*CUTS[g])
        if e in (2, 3, 8, 9):
            return got_z1.at[0, :, :, cols]
        if e in (0, 5, 6, 11):
            return small.at[0, 0, :, :, :, cols]
        return big.at[0, 0, :, :, :, :, cols]

    def arrive(k, e, g):
        held = bytes_of(e, g)
        pltpu.make_async_copy(held, held, recv_sem.at[k, e, g]).wait()

    def leave(k, e, g):
        held = bytes_of(e, g)
        pltpu.make_async_copy(held, held, send_sem.at[k, e, g]).wait()

    ring = range(1, SIDE)

    def plain(g):
        return pl.ds(*CUTS[g])

    def right(g):
        return pl.ds(half + CUTS[g][0], CUTS[g][1])

    def gather_first(k, e, g, buf):
        a, b = plain(g), right(g)
        for d in ring:
            send((k, e, g), buf.at[k, y, x, :, a], buf.at[k, y, x, :, a], device("x", d))
            send((k, e, g), buf.at[k, y, x, :, b], buf.at[k, y, x, :, b], device("y", d))

    def gather_second(k, e, g, buf):
        arrive(k, e - 1, g)
        a, b = plain(g), right(g)
        for d in ring:
            send((k, e, g), buf.at[k, y, :, :, a], buf.at[k, y, :, :, a], device("y", d))
            send((k, e, g), buf.at[k, :, x, :, b], buf.at[k, :, x, :, b], device("x", d))

    def scatter_first(k, e, g, i, src, weight, flipped, buf):
        a, b = plain(g), right(g)
        to_features(k, src, weight, flipped, buf, a)
        for d in ring:
            there = big.at[i, k, 0, d - 1, :, :, a]
            send((k, e, g), buf.at[k, at("y", d), :, :, a], there, device("y", d))
        to_features(k, src, weight, flipped, buf, b)
        for d in ring:
            there = big.at[i, k, 1, d - 1, :, :, a]
            send((k, e, g), buf.at[k, :, at("x", d), :, b], there, device("x", d))

    def scatter_second(k, e, g, i, buf):
        arrive(k, e - 1, g)
        a, b = plain(g), right(g)
        for n in range(SIDE):
            total = buf[k, y, n, :, a].astype(F32)
            for d in ring:
                total = total + big[i, k, 0, d - 1, n, :, a].astype(F32)
            sum_a[i, k, n, :, a] = total.astype(BF16)
        for d in ring:
            here = sum_a.at[i, k, at("x", d), :, a]
            send((k, e, g), here, small.at[i, k, 0, d - 1, :, a], device("x", d))
        for n in range(SIDE):
            total = buf[k, n, x, :, b].astype(F32)
            for d in ring:
                total = total + big[i, k, 1, d - 1, n, :, a].astype(F32)
            sum_b[i, k, n, :, a] = total.astype(BF16)
        for d in ring:
            here = sum_b.at[i, k, at("y", d), :, a]
            send((k, e, g), here, small.at[i, k, 1, d - 1, :, a], device("y", d))

    def scatter_total(k, e, g, i):
        arrive(k, e - 1, g)
        cols = plain(g)
        a = sum_a[i, k, x, :, cols].astype(F32)
        b = sum_b[i, k, y, :, cols].astype(F32)
        for d in ring:
            a = a + small[i, k, 0, d - 1, :, cols].astype(F32)
            b = b + small[i, k, 1, d - 1, :, cols].astype(F32)
        return (cols, a), (right(g), b)

    def col_scatter(k, e, g, src, weight, flipped, buf, got):
        cols = plain(g)
        to_units(k, src, weight, flipped, buf, cols)
        for d in ring:
            there = got.at[k, d - 1, :, cols]
            send((k, e, g), buf.at[k, at("z", d), :, cols], there, device("z", d))

    def col_total(k, e, g, buf, got):
        arrive(k, e - 1, g)
        cols = plain(g)
        total = buf[k, z, :, cols].astype(F32)
        for d in ring:
            total = total + got[k, d - 1, :, cols].astype(F32)
        return total

    def col_gather(k, e, g, buf):
        here = buf.at[k, z, :, plain(g)]
        for d in ring:
            send((k, e, g), here, here, device("z", d))

    def times(block, weight, flipped, cols):
        if flipped:
            return lax.dot_general(
                block, weight[cols, :], (((1,), (1,)), ((), ())), preferred_element_type=F32
            ).astype(BF16)
        return jnp.dot(block, weight[:, cols], preferred_element_type=F32).astype(BF16)

    def to_units(k, src, weight, flipped, dst, cols):
        value = times(src[k].reshape(rows, wide), weight, flipped, cols)
        dst[k, :, :, cols] = value.reshape(SIDE, rows // SIDE, cols.size)

    def to_features(k, src, weight, flipped, dst, cols):
        value = times(src[k].reshape(rows, units), weight, flipped, cols)
        dst[k, :, :, :, cols] = value.reshape(SIDE, SIDE, tokens, cols.size)

    def local(k):
        return pl.ds(k * tokens, tokens)

    everyone = CHUNKS * rows

    def weight_gradient(narrow, other_all, result, width):
        def tile(start, size):
            a = narrow[..., pl.ds(start, size)].reshape(everyone, size)
            b = other_all[...].reshape(everyone, width)
            result[pl.ds(start, size), :] = lax.dot_general(
                a, b, (((0,), (0,)), ((), ())), preferred_element_type=F32
            ).astype(BF16)

        return tile

    def event(k, e, g):
        groups = range(len(CUTS))
        if e in (2, 4, 8, 10):
            for other_g in groups:
                arrive(k, e - 1, other_g)
        if e == 0:
            gather_first(k, e, g, x_all)
        elif e == 1:
            gather_second(k, e, g, x_all)
        elif e == 2:
            for g in groups:
                col_scatter(k, e, g, x_all, w1, False, part1, got_z1)
        elif e == 3:
            value, slope = gelu_both(col_total(k, e, g, part1, got_z1))
            hidden_all[k, z, :, plain(g)] = value.astype(BF16)
            col_gather(k, e, g, hidden_all)
            dgelu[k, :, plain(g)] = slope
        elif e == 4:
            for g in groups:
                scatter_first(k, e, g, 0, hidden_all, w2, False, outp)
        elif e == 5:
            scatter_second(k, e, g, 0, outp)
        elif e == 6:
            for cols, total in scatter_total(k, e, g, 0):
                output = (x_ref[local(k), cols].astype(F32) + total).astype(BF16)
                out_ref[local(k), cols] = output
                slope = g_ref[local(k), cols].astype(F32) + feature_weight * (
                    output.astype(F32) - stale[local(k), cols].astype(F32)
                )
                slope_all[k, y, x, :, cols] = slope.astype(BF16)
            gather_first(k, e, g, slope_all)
        elif e == 7:
            gather_second(k, e, g, slope_all)
        elif e == 8:
            for g in groups:
                col_scatter(k, e, g, slope_all, w2, True, part2, got_z2)
        elif e == 9:
            inner = col_total(k, e, g, part2, got_z2) * dgelu[k, :, plain(g)]
            inner_all[k, z, :, plain(g)] = inner.astype(BF16)
            col_gather(k, e, g, inner_all)
        elif e == 10:
            for g in groups:
                scatter_first(k, e, g, 1, inner_all, w1, True, ginp)
        elif e == 11:
            scatter_second(k, e, g, 1, ginp)
        elif e == 12:
            for cols, total in scatter_total(k, e, g, 1):
                mine = slope_all[k, y, x, :, cols].astype(F32)
                gin_ref[local(k), cols] = (mine + total).astype(BF16)
        elif e == 13:
            column_tiles(g, units, weight_gradient(hidden_all, slope_all, gw2_ref, wide))
        elif e == 14:
            column_tiles(g, wide, weight_gradient(x_all, inner_all, gw1_ref, units))

    swap = pltpu.make_async_remote_copy(
        src_ref=s_ref, dst_ref=stale, send_sem=stale_sem.at[0], recv_sem=stale_sem.at[1],
        device_id=other, device_id_type=MESH,
    )
    once = {1: swap.start, 2: load1.wait, 4: load2.wait, 6: swap.wait_recv}
    for k, e, g in ORDER:
        if e in once:
            once.pop(e)()
        event(k, e, g)
    swap.wait_send()
    for k in range(CHUNKS):
        for e in range(STEPS):
            for g in range(len(CUTS)):
                leave(k, e, g)


def body(block_in, weight_in, weight_out, upstream, stale_out):
    x, w1, w2, g, s = block_in[0], weight_in[0], weight_out[0], upstream[0], stale_out[0]
    wide, units = w1.shape
    own = x.shape[0]
    tokens = own // CHUNKS
    rows = tokens * SIDE * SIDE
    half = wide // 2
    share = rows // SIDE
    ring = SIDE - 1
    inside = pl.BlockSpec(memory_space=pltpu.VMEM)
    anywhere = pl.BlockSpec(memory_space=pl.ANY)
    row_all = pltpu.VMEM((CHUNKS, SIDE, SIDE, tokens, wide), BF16)
    col_all = pltpu.VMEM((CHUNKS, SIDE, share, units), BF16)
    col_got = pltpu.VMEM((CHUNKS, ring, share, units), BF16)
    flops = 12 * own * 16 * wide * units
    out, gin, gw1, gw2 = pl.pallas_call(
        kernel,
        out_shape=(
            jax.ShapeDtypeStruct(x.shape, BF16),
            jax.ShapeDtypeStruct(x.shape, BF16),
            jax.ShapeDtypeStruct(w1.shape, BF16),
            jax.ShapeDtypeStruct(w2.shape, BF16),
        ),
        in_specs=[inside, inside, inside, anywhere, anywhere],
        out_specs=(inside,) * 4,
        scratch_shapes=[
            pltpu.VMEM((wide, units), BF16),
            pltpu.VMEM((units, wide), BF16),
            pltpu.VMEM(x.shape, BF16),
            row_all,
            row_all,
            col_all,
            col_all,
            pltpu.VMEM((CHUNKS, share, units), F32),
            col_all,
            col_all,
            col_got,
            col_got,
            row_all,
            row_all,
            pltpu.VMEM((2, CHUNKS, 2, ring, SIDE, tokens, half), BF16),
            pltpu.VMEM((2, CHUNKS, 2, ring, tokens, half), BF16),
            pltpu.VMEM((2, CHUNKS, SIDE, tokens, half), BF16),
            pltpu.VMEM((2, CHUNKS, SIDE, tokens, half), BF16),
            pltpu.SemaphoreType.DMA((CHUNKS, STEPS, len(CUTS))),
            pltpu.SemaphoreType.DMA((CHUNKS, STEPS, len(CUTS))),
            pltpu.SemaphoreType.DMA((2,)),
            pltpu.SemaphoreType.DMA((2,)),
        ],
        compiler_params=pltpu.CompilerParams(
            collective_id=0, has_side_effects=True, vmem_limit_bytes=44 << 20
        ),
        cost_estimate=pl.CostEstimate(
            flops=flops, bytes_accessed=8 * wide * units, transcendentals=0
        ),
    )(x, g, s, w1, w2)
    return out[None], gin[None], gw1[None], gw2[None]


def solution(mesh):
    placed = (
        P("peer", "row", "col"),
        P("peer", "col", "row"),
        P("peer", "row", "col"),
        P("peer", "row", "col"),
        P("peer", "row", "col"),
    )
    return jax.shard_map(
        body,
        mesh=mesh,
        in_specs=placed,
        out_specs=(
            P("peer", "row", "col"),
            P("peer", "row", "col"),
            P("peer", "col", "row"),
            P("peer", "row", "col"),
        ),
        check_vma=False,
    )
```
